256 devices in a mesh: row: 16 (over z, x_lo), col: 16 (over y, x_hi, core).
Axes of the slice: x: 4 (x_hi: 2, x_lo: 2; x = x_hi * 2 + x_lo), y: 4, z: 8, core: 2. Of those that a mesh axis runs over, the one named last changes fastest.
Arguments:
- object_slices: float32 [2, 4, 4096, 4096], P(None, None, 'row', 'col'), may hold values from -1 to 1
- positions: int32 [16, 16, 2, 2], P('row', 'col'), may hold values from 0 to 128
- intensities: float32 [16, 16, 2, 256, 256], P('row', 'col'), may hold values from 0 to 0.8
- probe: float32 [2, 256, 256], replicated, may hold values from -6 to 6
- propagator: float32 [256, 256], replicated, may hold values from -3.140625 to 3.140625
Outputs:
- gradient: float32 [2, 4, 4096, 4096], P(None, None, 'row', 'col')
- updated: float32 [2, 4, 4096, 4096], P(None, None, 'row', 'col')
The draws below stay inside these ranges and needn't reach their ends.
Inputs may be any that keep to these rules, and one draw needn't show every extreme that they name: `positions`: each probe window lies inside its tile widened by 64 pixels on every side.
All inputs are finite; a program needn't handle non-finite values.
Results may differ from the reference program's by a relative error of at most 0.0003.
Values sent between devices are 32-bit elements; how exact they have to be, the bound alone decides.
No kernel may reach another device: no remote copies, remote signals or barrier semaphores. Data moves between devices by JAX's collectives and lax.ppermute only.
A program may use at most 128 MiB of HBM per device.

```python
import jax
import jax.numpy as jnp
from jax import lax

CORE = 256
HALO = 64
W = 256
SLICES = 4
PROBES = 2
NY = 4096
NX = 4096
N_ROW = 16
N_COL = 16


def plant(entries, rng, smallest, high):
    shape = entries.shape
    place = [jax.random.randint(jax.random.fold_in(rng, axis), (), 0, shape[axis]) for axis in range(len(shape))]
    entries = entries.at[tuple(place)].set(smallest)
    longest = shape.index(max(shape))
    place[longest] = (place[longest] + 1) % shape[longest]
    return entries.at[tuple(place)].set(high)


def block_scale(stream_key, dims, split, low, top_value):
    gain, own = 1.0, jax.random.fold_in(stream_key, 6)
    for axis_at, shards_of in split:
        heights = jnp.exp(jax.random.uniform(jax.random.fold_in(own, axis_at), (shards_of,), jnp.float32, low / len(split), top_value / len(split)))
        gain = gain * jnp.repeat(heights, dims[axis_at] // shards_of).reshape([-1 if axis == axis_at else 1 for axis in range(len(dims))])
    return gain


def bell_draw(rng, extent, scale, limit, held_as=jnp.bfloat16):
    array = jax.random.normal(rng, extent, jnp.float32) * scale
    return jnp.minimum(jnp.maximum(array, -limit), limit).astype(held_as)


def setup_inputs(seed: int = 0) -> dict:
    splits = jax.random.split(jax.random.key(seed), 6)
    object_slices = jnp.clip(jax.random.uniform(splits[0], (2, SLICES, NY, NX), jnp.float32, -1.0, 1.0) * block_scale(splits[0], (2, SLICES, NY, NX), ((2, 16), (3, 16)), -0.4, 0.0), -1.0, 1.0)
    positions = plant(jax.random.randint(splits[1], (N_ROW, N_COL, PROBES, 2), 0, CORE + 2 * HALO - W + 1), jax.random.fold_in(splits[1], 1), 0, CORE + 2 * HALO - W).astype(jnp.int32)
    intensities = jnp.clip(0.8 * jax.random.uniform(splits[2], (N_ROW, N_COL, PROBES, W, W), jnp.float32) ** block_scale(splits[2], (N_ROW, N_COL, PROBES, W, W), ((0, 16), (1, 16)), -0.2, 0.2), 0.0, 0.8)
    probe = bell_draw(splits[3], (2, W, W), 1.0, 6.0, jnp.float32)
    propagator = jnp.clip(jax.random.uniform(splits[4], (W, W), jnp.float32, -3.140625, 3.140625), -3.140625, 3.140625)
    return {"object_slices": object_slices, "positions": positions, "intensities": intensities, "probe": probe, "propagator": propagator}


descent_rate = 0.5

def tables(width):
    counter = jnp.arange(width, dtype=jnp.int32)
    product = counter[:, None] * counter[None, :] % width
    angles = product.astype(jnp.float32) * (2.0 * jnp.pi / width)
    norming = 1.0 / jnp.sqrt(jnp.float32(width))
    return (jnp.cos(angles) * norming, jnp.sin(angles) * norming)

def apply_left(matrix, field):
    return jnp.einsum('ab,kbc->kac', matrix, field, precision=lax.Precision.HIGHEST)

def apply_right(field, matrix):
    return jnp.einsum('kab,bc->kac', field, matrix, precision=lax.Precision.HIGHEST)

def fourier(real_part, imag_part, cosines, sines, direction):
    half_re = apply_left(cosines, real_part) - direction * apply_left(sines, imag_part)
    half_im = apply_left(cosines, imag_part) + direction * apply_left(sines, real_part)
    full_re = apply_right(half_re, cosines) - direction * apply_right(half_im, sines)
    full_im = apply_right(half_im, cosines) + direction * apply_right(half_re, sines)
    return (full_re, full_im)

def complex_product(left_re, left_im, right_re, right_im):
    return (left_re * right_re - left_im * right_im, left_re * right_im + left_im * right_re)

def probe_gradients(windows, probe, propagator, measured):
    width = probe.shape[-1]
    layers = windows.shape[2]
    count = windows.shape[0]
    cosines, sines = tables(width)
    phase_re = jnp.cos(propagator)
    phase_im = jnp.sin(propagator)
    wave_re = jnp.broadcast_to(probe[0], (count, width, width))
    wave_im = jnp.broadcast_to(probe[1], (count, width, width))
    stored = []
    for layer in range(layers):
        stored.append((wave_re, wave_im))
        exit_re, exit_im = complex_product(wave_re, wave_im, windows[:, 0, layer], windows[:, 1, layer])
        if layer < layers - 1:
            freq_re, freq_im = fourier(exit_re, exit_im, cosines, sines, -1.0)
            freq_re, freq_im = complex_product(freq_re, freq_im, phase_re, phase_im)
            wave_re, wave_im = fourier(freq_re, freq_im, cosines, sines, 1.0)
    far_re, far_im = fourier(exit_re, exit_im, cosines, sines, -1.0)
    misfit = far_re * far_re + far_im * far_im - measured
    back_re, back_im = fourier(misfit * far_re, misfit * far_im, cosines, sines, 1.0)
    real_terms = [None] * layers
    imag_terms = [None] * layers
    for layer in range(layers - 1, -1, -1):
        wave_re, wave_im = stored[layer]
        real_terms[layer] = wave_re * back_re + wave_im * back_im
        imag_terms[layer] = wave_re * back_im - wave_im * back_re
        if layer > 0:
            slab_re = windows[:, 0, layer]
            slab_im = windows[:, 1, layer]
            back_re, back_im = (slab_re * back_re + slab_im * back_im, slab_re * back_im - slab_im * back_re)
            freq_re, freq_im = fourier(back_re, back_im, cosines, sines, -1.0)
            freq_re, freq_im = complex_product(freq_re, freq_im, phase_re, -phase_im)
            back_re, back_im = fourier(freq_re, freq_im, cosines, sines, 1.0)
    real_stack = jnp.stack(real_terms, axis=1)
    imag_stack = jnp.stack(imag_terms, axis=1)
    return jnp.stack([real_stack, imag_stack], axis=1)

def reference(object_slices, positions, intensities, probe, propagator):
    total_rows = object_slices.shape[2]
    total_cols = object_slices.shape[3]
    width = probe.shape[-1]
    counter = jnp.arange(width, dtype=jnp.int32)

    def cut_window(row_index, col_index):
        return object_slices[:, :, row_index][:, :, :, col_index]

    def one_tile(gradient_sum, tile_index):
        tile_row = tile_index // N_COL
        tile_col = tile_index % N_COL
        offsets = positions[tile_row, tile_col]
        row_start = tile_row * CORE - HALO + offsets[:, 0]
        col_start = tile_col * CORE - HALO + offsets[:, 1]
        row_index = ((row_start[:, None] + counter[None, :]) % total_rows).astype(jnp.int32)
        col_index = ((col_start[:, None] + counter[None, :]) % total_cols).astype(jnp.int32)
        windows = jax.vmap(cut_window)(row_index, col_index)
        terms = probe_gradients(windows, probe, propagator, intensities[tile_row, tile_col])

        def add_one(index, running):
            return running.at[:, :, row_index[index][:, None], col_index[index][None, :]].add(terms[index])
        gradient_sum = lax.fori_loop(0, terms.shape[0], add_one, gradient_sum)
        return (gradient_sum, None)
    zeros = jnp.zeros_like(object_slices)
    gradient, _ = lax.scan(one_tile, zeros, jnp.arange(N_ROW * N_COL, dtype=jnp.int32))
    return (gradient, object_slices - descent_rate * gradient)
```

```python
import functools

import jax
import jax.numpy as jnp
import ml_dtypes
import numpy as np
from jax import lax
from jax.experimental import pallas as pl
from jax.experimental.pallas import tpu as pltpu
from jax.sharding import PartitionSpec as P

HALO = 64
W = 256
HALF = 128
F32 = jnp.float32
BF16 = jnp.bfloat16
AXES = ("row", "col")
FIRST = (0, 1, 2)
LAST = (3,)
RATE = 0.5


def fourier_tables():
    n = np.arange(HALF)
    angle = 2.0 * np.pi * (np.outer(n, n) % HALF) / HALF
    cos, sin = np.cos(angle) / 16.0, np.sin(angle) / 16.0
    forward = np.block([[cos, sin], [-sin, cos]]).astype(np.float32)
    both = []
    for matrix in (forward, forward.T):
        high = matrix.astype(ml_dtypes.bfloat16)
        low = (matrix - high.astype(np.float32)).astype(ml_dtypes.bfloat16)
        both += [high, low]
    matrices = np.stack(both)
    turn = 2.0 * np.pi * n / W
    twiddle = np.stack([np.cos(turn), np.sin(turn)]).astype(np.float32)
    by_row = np.broadcast_to(twiddle[:, :, None], (2, HALF, HALF)).copy()
    by_lane = np.broadcast_to(twiddle[:, None, :], (2, 8, HALF)).copy()
    order = np.zeros((W, W), np.float32)
    order[2 * n, n] = 1.0
    order[2 * n + 1, HALF + n] = 1.0
    return matrices, by_row, by_lane, np.stack([order.T, order]).astype(ml_dtypes.bfloat16)


def lanes(rows):
    return lax.broadcasted_iota(jnp.int32, (rows, HALF), 1)


def rows_of(first, rows):
    return first + lax.broadcasted_iota(jnp.int32, (rows, HALF), 0)


def swap(x):
    return pltpu.roll(x, HALO, 1)


def split(x):
    high = x.astype(BF16)
    return high, (x - high.astype(F32)).astype(BF16)


def mul(ar, ai, br, bi):
    return ar * br - ai * bi, ar * bi + ai * br


def mul_conj(ar, ai, br, bi):
    return ar * br + ai * bi, ar * bi - ai * br


def dot(a, b):
    return jnp.dot(a, b, preferred_element_type=F32)


def pack_left(re0, im0):
    low = lanes(re0.shape[0]) < HALO
    return jnp.where(low, re0, swap(im0))


def pack_right(re1, im1):
    low = lanes(re1.shape[0]) < HALO
    return jnp.where(low, swap(im1), re1)


def columns_out(core_ref, object_ref, out_ref):
    core = core_ref[0]
    for s in range(4):
        for r in range(0, W, 64):
            rows = pl.ds(r, 64)
            left = pack_left(object_ref[0, s, rows, :HALF], object_ref[1, s, rows, :HALF])
            right = pack_right(object_ref[0, s, rows, HALF:], object_ref[1, s, rows, HALF:])
            out_ref[s, rows, :] = jnp.where(core == 1, right, left)


def columns_in(slices, core_ref, object_ref, below_ref, above_ref, out_ref):
    core = core_ref[0]
    for j, s in enumerate(slices):
        for r in range(0, 384, 64):
            if r < W:
                re, im = object_ref[0, s, r : r + 64], object_ref[1, s, r : r + 64]
            else:
                ref = below_ref if r == W else above_ref
                re, im = ref[0, j], ref[1, j]
            left = pack_left(re[:, :HALF], im[:, :HALF])
            right = pack_right(re[:, HALF:], im[:, HALF:])
            out_ref[j, r : r + 64, :] = jnp.where(core == 1, left, right)


def prepare(pos_ref, probe_ref, propagator_ref, intensity_ref, order_ref, wave_ref, phase_ref, measured_ref):
    for k in range(2):
        a = lax.rem(pos_ref[k, 0] + (W - HALO), W)
        b = lax.rem(pos_ref[k, 1] + (W - HALO), W)
        for c in range(2):
            wave_ref[k, c] = pltpu.roll(pltpu.roll(probe_ref[c], a, 0), b, 1)

    def ordered(x):
        for left in (True, False):
            total = None
            for _ in range(3):
                part = x.astype(BF16)
                x = x - part.astype(F32)
                term = dot(order_ref[0], part) if left else dot(part, order_ref[1])
                total = term if total is None else total + term
            x = total
        return x

    angle = ordered(propagator_ref[...])
    phase_ref[0] = jnp.cos(angle)
    phase_ref[1] = jnp.sin(angle)
    for k in range(2):
        measured_ref[k] = ordered(intensity_ref[k])


STEP = 32


class Transform:
    def __init__(self, tables, scratch):
        self.matrices, self.by_row, self.by_lane = tables
        self.xr_h, self.xr_l, self.xl_h, self.xl_l, self.wr, self.wl = scratch

    def put_rows(self, k, e, r, re, im):
        cols = slice(e * W, (e + 1) * W)
        n = re.shape[0]
        for base, x in ((0, re), (HALF, im)):
            high, low = split(x)
            self.xr_h[k, base + r : base + r + n, cols] = high
            self.xr_l[k, base + r : base + r + n, cols] = low

    def put_lanes(self, k, e, r, re, im):
        n = re.shape[0]
        for base, x in ((0, re), (HALF, im)):
            high, low = split(x)
            self.xl_h[k, e * W + r : e * W + r + n, base : base + HALF] = high
            self.xl_l[k, e * W + r : e * W + r + n, base : base + HALF] = low

    def enter(self, k, r, n, first, second):
        c = jnp.concatenate([self.by_row[0, r : r + n, :]] * 2, axis=1)
        s = jnp.concatenate([self.by_row[1, r : r + n, :]] * 2, axis=1)
        self.put_rows(k, 0, r, first[0] + second[0], first[1] + second[1])
        dr, di = first[0] - second[0], first[1] - second[1]
        self.put_rows(k, 1, r, dr * c + di * s, di * c - dr * s)

    def dot_rows(self, k, inverse):
        high, low = self.matrices[2 * inverse], self.matrices[2 * inverse + 1]
        xh, xl = self.xr_h[k], self.xr_l[k]
        self.wr[k] = dot(high, xh) + dot(high, xl) + dot(low, xh)

    def dot_lanes(self, k, inverse):
        high, low = self.matrices[2 - 2 * inverse], self.matrices[3 - 2 * inverse]
        xh, xl = self.xl_h[k], self.xl_l[k]
        self.wl[k] = dot(xh, high) + dot(xl, high) + dot(xh, low)

    def forward(self, k):
        self.dot_rows(k, 0)
        for e in range(2):
            cols = slice(e * W, (e + 1) * W)
            for r in range(0, HALF, STEP):
                n = STEP
                re = self.wr[k, r : r + n, cols]
                im = self.wr[k, HALF + r : HALF + r + n, cols]
                row = e * HALF + r
                c = jnp.concatenate([self.by_lane[0]] * (n // 8), axis=0)
                s = jnp.concatenate([self.by_lane[1]] * (n // 8), axis=0)
                re0, re1, im0, im1 = re[:, :HALF], re[:, HALF:], im[:, :HALF], im[:, HALF:]
                self.put_lanes(k, 0, row, re0 + re1, im0 + im1)
                dr, di = re0 - re1, im0 - im1
                self.put_lanes(k, 1, row, dr * c + di * s, di * c - dr * s)
        self.dot_lanes(k, 0)

    def modify(self, k, change):
        for e in range(2):
            for r in range(0, W, STEP):
                n = STEP
                rows = slice(e * W + r, e * W + r + n)
                re, im = change(e, slice(r, r + n), self.wl[k, rows, :HALF], self.wl[k, rows, HALF:])
                self.put_lanes(k, e, r, re, im)

    def backward(self, k):
        self.dot_lanes(k, 1)
        for e in range(2):
            for r in range(0, HALF, STEP):
                n = STEP
                row = e * HALF + r
                c = jnp.concatenate([self.by_lane[0]] * (n // 8), axis=0)
                s = jnp.concatenate([self.by_lane[1]] * (n // 8), axis=0)
                er, ei = self.wl[k, row : row + n, :HALF], self.wl[k, row : row + n, HALF:]
                tr, ti = self.wl[k, W + row : W + row + n, :HALF], self.wl[k, W + row : W + row + n, HALF:]
                tr, ti = tr * c - ti * s, ti * c + tr * s
                re = jnp.concatenate([er + tr, er - tr], axis=1)
                im = jnp.concatenate([ei + ti, ei - ti], axis=1)
                self.put_rows(k, e, r, re, im)
        self.dot_rows(k, 1)

    def leave(self, k, r, n):
        c = jnp.concatenate([self.by_row[0, r : r + n, :]] * 2, axis=1)
        s = jnp.concatenate([self.by_row[1, r : r + n, :]] * 2, axis=1)
        er, ei = self.wr[k, r : r + n, :W], self.wr[k, HALF + r : HALF + r + n, :W]
        tr, ti = self.wr[k, r : r + n, W:], self.wr[k, HALF + r : HALF + r + n, W:]
        tr, ti = tr * c - ti * s, ti * c + tr * s
        return (er + tr, ei + ti), (er - tr, ei - ti)


def phase_of(phase_ref, sign):
    def change(e, rows, re, im):
        cols = slice(e * HALF, (e + 1) * HALF)
        pr, pi = phase_ref[0, rows, cols], phase_ref[1, rows, cols]
        return mul(re, im, pr, pi) if sign > 0 else mul_conj(pr, pi, re, im)

    return change


def misfit_of(measured_ref, k):
    def change(e, rows, re, im):
        cols = slice(e * HALF, (e + 1) * HALF)
        misfit = re * re + im * im - measured_ref[k, rows, cols]
        return misfit * re, misfit * im

    return change


class Windows:
    def __init__(self, pos_ref, core_ref, refs, side):
        self.core = core_ref[0]
        self.object, self.below, self.above, self.out, self.out_below, self.out_above, self.inner = refs
        self.side = side
        self.shift = [(pos_ref[k, 0] - HALO, pos_ref[k, 1] - HALO) for k in range(2)]

    def gather_sides(self, j):
        for r in range(0, 384, 64):
            if r < W:
                outer = self.out[j, r : r + 64]
            else:
                outer = (self.out_below if r == W else self.out_above)[j]
            inner = self.inner[j, r : r + 64]
            right = jnp.where(self.core == 1, outer, inner)
            left = jnp.where(self.core == 1, inner, outer)
            low = lanes(64) < HALO
            self.side[0, r : r + 64] = jnp.where(low, right, left)
            self.side[1, r : r + 64] = swap(jnp.where(low, left, right))

    def with_sides(self, k, own, side):
        b = self.shift[k][1]
        lane = lanes(own.shape[0])
        return (
            jnp.where(lane < b, side, own[:, :HALF]),
            jnp.where(lane >= HALF + b, side, own[:, HALF:]),
        )

    def window(self, s, j, k, c, r, n):
        tiles = self.with_sides(k, self.object[c, s, r : r + n, :], self.side[c, r : r + n])
        a = self.shift[k][0]
        if r < HALO:
            other = self.with_sides(k, self.below[c, j, r : r + n, :], self.side[c, W + r : W + r + n])
            wraps = rows_of(r, n) < a
        elif r >= W - HALO:
            q = r - (W - HALO)
            other = self.with_sides(k, self.above[c, j, q : q + n, :], self.side[c, W + HALO + q : W + HALO + q + n])
            wraps = rows_of(r, n) >= W + a
        else:
            return jnp.concatenate(tiles, axis=1)
        return jnp.concatenate([jnp.where(wraps, o, t) for t, o in zip(tiles, other)], axis=1)


class Folding:
    def __init__(self, pos_ref, core_ref, refs):
        self.core = core_ref[0]
        self.own, self.below, self.above, self.out, self.out_below, self.out_above, self.inner = refs
        self.shift = [(pos_ref[k, 0] - HALO, pos_ref[k, 1] - HALO) for k in range(2)]

    def part(self, terms, keep):
        n = terms[0].shape[0]
        lane = lanes(n)
        tiles, sides = [0.0, 0.0], 0.0
        for k, term in enumerate(terms):
            b = self.shift[k][1]
            zero = jnp.zeros((n, HALF), F32)
            for t, wraps in enumerate((lane < b, lane >= HALF + b)):
                x = term[:, t * HALF : (t + 1) * HALF]
                if keep is not None:
                    x = jnp.where(keep[k], x, zero)
                tiles[t] = tiles[t] + jnp.where(wraps, zero, x)
                sides = sides + jnp.where(wraps, x, zero)
        return jnp.concatenate(tiles, axis=1), sides

    def sides_to(self, j, r, n, re, im, out):
        low = lanes(n) < HALO
        flipped = swap(im)
        right = jnp.where(low, re, flipped)
        left = jnp.where(low, flipped, re)
        ref, at = out
        ref[j, at : at + n] = jnp.where(self.core == 1, right, left)
        self.inner[j, r : r + n] = jnp.where(self.core == 1, left, right)

    def put(self, j, r, terms):
        n = terms[0][0].shape[0]
        if HALO <= r < W - HALO:
            parts = [self.part(terms[c], None) for c in range(2)]
        else:
            row = rows_of(r, n)
            if r < HALO:
                wraps = [row < self.shift[k][0] for k in range(2)]
                band, out, at, q = self.below, self.out_below, r, W + r
            else:
                wraps = [row >= W + self.shift[k][0] for k in range(2)]
                at = r - (W - HALO)
                band, out, q = self.above, self.out_above, W + HALO + at
            away = [self.part(terms[c], wraps) for c in range(2)]
            for c in range(2):
                band[c, j, at : at + n, :] = away[c][0]
            self.sides_to(j, q, n, away[0][1], away[1][1], (out, at))
            stays = [jnp.logical_not(w) for w in wraps]
            parts = [self.part(terms[c], stays) for c in range(2)]
        for c in range(2):
            self.own[c, j, r : r + n, :] = parts[c][0]
        self.sides_to(j, r, n, parts[0][1], parts[1][1], (self.out, r))


PAIRS = [(r, STEP) for r in range(0, HALF, STEP)]


def forward_kernel(pos, core, wave0, phase, obj, below, above, out, out_below, out_above, inner, mats, by_row, by_lane,
                   waves, seen, xr_h, xr_l, xl_h, xl_l, wr, wl, side):
    t = Transform((mats, by_row, by_lane), (xr_h, xr_l, xl_h, xl_l, wr, wl))
    w = Windows(pos, core, (obj, below, above, out, out_below, out_above, inner), side)
    for s in range(3):
        w.gather_sides(s)
        for k in range(2):
            for r, n in PAIRS:
                if s:
                    pair = t.leave(k, r, n)
                else:
                    pair = [(wave0[k, 0, q : q + n, :], wave0[k, 1, q : q + n, :]) for q in (r, r + HALF)]
                exits = []
                for q, (re, im) in zip((r, r + HALF), pair):
                    o = [w.window(s, s, k, c, q, n) for c in range(2)]
                    if s:
                        for c, x in enumerate((re, im)):
                            waves[s - 1, k, c, q : q + n, :] = x
                            seen[s - 1, k, c, q : q + n, :] = o[c]
                    exits.append(mul(re, im, *o))
                t.enter(k, r, n, *exits)
        for k in range(2):
            t.forward(k)
        for k in range(2):
            t.modify(k, phase_of(phase, 1))
        for k in range(2):
            t.backward(k)
    for k in range(2):
        for r, n in PAIRS:
            for q, pair in zip((r, r + HALF), t.leave(k, r, n)):
                for c in range(2):
                    waves[2, k, c, q : q + n, :] = pair[c]


def turn_kernel(pos, core, waves, measured, obj, below, above, out, out_below, out_above, inner, mats, by_row, by_lane,
                back, own, g_below, g_above, g_out, g_out_below, g_out_above, g_inner,
                xr_h, xr_l, xl_h, xl_l, wr, wl, side):
    t = Transform((mats, by_row, by_lane), (xr_h, xr_l, xl_h, xl_l, wr, wl))
    w = Windows(pos, core, (obj, below, above, out, out_below, out_above, inner), side)
    f = Folding(pos, core, (own, g_below, g_above, g_out, g_out_below, g_out_above, g_inner))
    w.gather_sides(0)
    for k in range(2):
        for r, n in PAIRS:
            exits = []
            for q in (r, r + HALF):
                o = [w.window(3, 0, k, c, q, n) for c in range(2)]
                for c in range(2):
                    back[k, c, q : q + n, :] = o[c]
                exits.append(mul(waves[2, k, 0, q : q + n, :], waves[2, k, 1, q : q + n, :], *o))
            t.enter(k, r, n, *exits)
    for k in range(2):
        t.forward(k)
    for k in range(2):
        t.modify(k, misfit_of(measured, k))
    for k in range(2):
        t.backward(k)
    for r, n in PAIRS:
        pairs = [t.leave(k, r, n) for k in range(2)]
        for half, q in enumerate((r, r + HALF)):
            terms = [[], []]
            for k in range(2):
                g = pairs[k][half]
                term = mul_conj(waves[2, k, 0, q : q + n, :], waves[2, k, 1, q : q + n, :], *g)
                for c in range(2):
                    terms[c].append(term[c])
                o = back[k, 0, q : q + n, :], back[k, 1, q : q + n, :]
                back[k, 0, q : q + n, :], back[k, 1, q : q + n, :] = mul_conj(*o, *g)
            f.put(0, q, terms)


def backward_kernel(pos, core, back, wave0, waves, seen, phase, mats, by_row, by_lane,
                    own, g_below, g_above, g_out, g_out_below, g_out_above, g_inner,
                    xr_h, xr_l, xl_h, xl_l, wr, wl):
    t = Transform((mats, by_row, by_lane), (xr_h, xr_l, xl_h, xl_l, wr, wl))
    f = Folding(pos, core, (own, g_below, g_above, g_out, g_out_below, g_out_above, g_inner))
    for k in range(2):
        for r, n in PAIRS:
            t.enter(k, r, n, *[(back[k, 0, q : q + n, :], back[k, 1, q : q + n, :]) for q in (r, r + HALF)])
    for s in (2, 1, 0):
        for k in range(2):
            t.forward(k)
        for k in range(2):
            t.modify(k, phase_of(phase, -1))
        for k in range(2):
            t.backward(k)
        for r, n in PAIRS:
            pairs = [t.leave(k, r, n) for k in range(2)]
            for half, q in enumerate((r, r + HALF)):
                terms = [[], []]
                for k in range(2):
                    wave = (
                        (waves[s - 1, k, 0, q : q + n, :], waves[s - 1, k, 1, q : q + n, :])
                        if s
                        else (wave0[k, 0, q : q + n, :], wave0[k, 1, q : q + n, :])
                    )
                    term = mul_conj(*wave, *pairs[k][half])
                    for c in range(2):
                        terms[c].append(term[c])
                f.put(s, q, terms)
            if s:
                for k in range(2):
                    exits = [
                        mul_conj(seen[s - 1, k, 0, q : q + n, :], seen[s - 1, k, 1, q : q + n, :], *pairs[k][half])
                        for half, q in enumerate((r, r + HALF))
                    ]
                    t.enter(k, r, n, *exits)


def spread(core, outer, inner):
    low = lanes(outer.shape[0]) < HALO
    zero = jnp.zeros(outer.shape, F32)
    left = jnp.where(core == 1, inner, outer)
    right = jnp.where(core == 1, outer, inner)
    left_im, right_im = swap(left), swap(right)
    re = jnp.concatenate([jnp.where(low, left, zero), jnp.where(low, zero, right)], axis=1)
    im = jnp.concatenate([jnp.where(low, left_im, zero), jnp.where(low, zero, right_im)], axis=1)
    return re, im


def bands_kernel(count, core_ref, g_below, g_above, inner, to_below, to_above):
    core = core_ref[0]
    for j in range(count):
        for at, source, target in ((W, g_below, to_below), (W + HALO, g_above, to_above)):
            part = inner[j, at : at + HALO]
            more = spread(core, jnp.zeros_like(part), part)
            for c in range(2):
                target[c, j] = source[c, j] + more[c]


def final_kernel(core_ref, obj, *refs):
    core = core_ref[0]
    groups = (refs[0:7], refs[7:14])
    gradient, updated = refs[14:]
    for slices, (own, from_above, from_below, out, out_above, out_below, inner) in zip((FIRST, LAST), groups):
        for j, s in enumerate(slices):
            for r in range(0, W, 64):
                side = out[j, r : r + 64]
                if r == 0:
                    side = side + out_above[j]
                if r == W - HALO:
                    side = side + out_below[j]
                more = spread(core, side, inner[j, r : r + 64])
                for c in range(2):
                    total = own[c, j, r : r + 64, :] + more[c]
                    if r == 0:
                        total = total + from_above[c, j]
                    if r == W - HALO:
                        total = total + from_below[c, j]
                    gradient[c, s, r : r + 64, :] = total
                    updated[c, s, r : r + 64, :] = obj[c, s, r : r + 64, :] - RATE * total


def call(kernel, outs, args, scalars, scratch=(), flops=0, moved=0, limit=24):
    smem = pl.BlockSpec(memory_space=pltpu.SMEM)
    vmem = pl.BlockSpec(memory_space=pltpu.VMEM)
    shapes = [jax.ShapeDtypeStruct(shape, F32) for shape in outs]
    return pl.pallas_call(
        kernel,
        out_shape=shapes,
        in_specs=[smem] * scalars + [vmem] * (len(args) - scalars),
        out_specs=[vmem] * len(shapes),
        scratch_shapes=list(scratch),
        compiler_params=pltpu.CompilerParams(vmem_limit_bytes=limit * 1024 * 1024),
        cost_estimate=pl.CostEstimate(flops=flops, bytes_accessed=moved, transcendentals=0),
    )(*args)


TRANSFORM_SCRATCH = [
    pltpu.VMEM((2, W, 2 * W), BF16),
    pltpu.VMEM((2, W, 2 * W), BF16),
    pltpu.VMEM((2, 2 * W, W), BF16),
    pltpu.VMEM((2, 2 * W, W), BF16),
    pltpu.VMEM((2, W, 2 * W), F32),
    pltpu.VMEM((2, 2 * W, W), F32),
]
SIDE_SCRATCH = pltpu.VMEM((2, 384, HALF), F32)


def routes(rows, cols):
    def out(c):
        return c + 1 if c % 2 else c - 1

    def build(step, col):
        return [
            (r * cols + c, (r + step) % rows * cols + col(c) % cols) for r in range(rows) for c in range(cols)
        ]

    return {
        "up": build(-1, lambda c: c),
        "down": build(1, lambda c: c),
        "out": build(0, out),
        "out_up": build(-1, out),
        "out_down": build(1, out),
        "in": build(0, lambda c: c - 1 if c % 2 else c + 1),
    }


def on_device(obj, positions, intensities, probe, propagator, *, route):
    matrices, by_row, by_lane, order = (jnp.asarray(x) for x in fourier_tables())
    tables = (matrices, by_row, by_lane)
    core = (lax.axis_index("col") % 2).astype(jnp.int32).reshape(1)
    pos = positions[0, 0]

    def send(x, way):
        return lax.ppermute(x, AXES, route[way])

    halo = []
    bands = {}
    for name, slices in (("first", FIRST), ("last", LAST)):
        lo, hi = slices[0], slices[-1] + 1
        bands[name] = (send(obj[:, lo:hi, :HALO], "up"), send(obj[:, lo:hi, W - HALO :], "down"))
    (packed,) = call(columns_out, [(4, W, HALF)], (core, obj), 1)
    wave0, phase, measured = call(
        prepare,
        [(2, 2, W, W), (2, W, W), (2, W, W)],
        (pos, probe, propagator, intensities[0, 0], order),
        1,
    )
    for name, slices in (("first", FIRST), ("last", LAST)):
        lo, hi = slices[0], slices[-1] + 1
        below, above = bands[name]
        out = send(packed[lo:hi], "out")
        out_below = send(packed[lo:hi, :HALO], "out_up")
        out_above = send(packed[lo:hi, W - HALO :], "out_down")
        (inward,) = call(
            functools.partial(columns_in, slices), [(len(slices), 384, HALF)], (core, obj, below, above), 1
        )
        halo.append((below, above, out, out_below, out_above, send(inward, "in")))

    def term_shapes(n):
        return [
            (2, n, W, W),
            (2, n, HALO, W),
            (2, n, HALO, W),
            (n, W, HALF),
            (n, HALO, HALF),
            (n, HALO, HALF),
            (n, 384, HALF),
        ]

    flops = 2 * 2 * 8 * 3 * 2 * W**3 // 2
    waves, seen = call(
        forward_kernel,
        [(3, 2, 2, W, W), (2, 2, 2, W, W)],
        (pos, core, wave0, phase, obj, *halo[0], *tables),
        2,
        TRANSFORM_SCRATCH + [SIDE_SCRATCH],
        flops=3 * flops,
        moved=2**23,
    )
    back, *last = call(
        turn_kernel,
        [(2, 2, W, W)] + term_shapes(1),
        (pos, core, waves, measured, obj, *halo[1], *tables),
        2,
        TRANSFORM_SCRATCH + [SIDE_SCRATCH],
        flops=flops,
        moved=2**23,
    )
    first = call(
        backward_kernel,
        term_shapes(3),
        (pos, core, back, wave0, waves, seen, phase, *tables),
        2,
        TRANSFORM_SCRATCH,
        flops=3 * flops,
        moved=2**23,
    )

    received = []
    for terms, n in ((last, 1), (first, 3)):
        own, g_below, g_above, g_out, g_out_below, g_out_above, g_inner = terms
        inner = send(g_inner, "in")
        out = send(g_out, "out")
        out_above = send(g_out_below, "out_down")
        out_below = send(g_out_above, "out_up")
        to_below, to_above = call(
            functools.partial(bands_kernel, n), term_shapes(n)[1:3], (core, g_below, g_above, inner), 1
        )
        from_above = send(to_below, "down")
        from_below = send(to_above, "up")
        received.append((own, from_above, from_below, out, out_above, out_below, inner))
    return tuple(
        call(final_kernel, [(2, 4, W, W)] * 2, (core, obj, *received[1], *received[0]), 1, limit=24)
    )


def solution(mesh):
    route = routes(mesh.shape["row"], mesh.shape["col"])
    return jax.shard_map(
        functools.partial(on_device, route=route),
        mesh=mesh,
        in_specs=(
            P(None, None, "row", "col"),
            P("row", "col", None, None),
            P("row", "col", None, None, None),
            P(),
            P(),
        ),
        out_specs=(P(None, None, "row", "col"), P(None, None, "row", "col")),
        check_vma=False,
    )
```

```python
import functools

import jax
import jax.numpy as jnp
import ml_dtypes
import numpy as np
from jax import lax
from jax.experimental import pallas as pl
from jax.experimental.pallas import tpu as pltpu
from jax.sharding import PartitionSpec as P

HALO = 64
W = 256
HALF = 128
F32 = jnp.float32
BF16 = jnp.bfloat16
AXES = ("row", "col")
RATE = 0.5
PARTED = 2


def fourier_tables():
    n = np.arange(HALF)
    angle = 2.0 * np.pi * (np.outer(n, n) % HALF) / HALF
    cos, sin = np.cos(angle) / 16.0, np.sin(angle) / 16.0
    forward = np.block([[cos, sin], [-sin, cos]]).astype(np.float32)
    both = []
    for matrix in (forward, forward.T):
        high = matrix.astype(ml_dtypes.bfloat16)
        low = (matrix - high.astype(np.float32)).astype(ml_dtypes.bfloat16)
        both += [high, low]
    matrices = np.stack(both)
    turn = 2.0 * np.pi * n / W
    twiddle = np.stack([np.cos(turn), np.sin(turn)]).astype(np.float32)
    by_row = np.broadcast_to(twiddle[:, :, None], (2, HALF, HALF)).copy()
    by_lane = np.broadcast_to(twiddle[:, None, :], (2, 8, HALF)).copy()
    order = np.zeros((W, W), np.float32)
    order[2 * n, n] = 1.0
    order[2 * n + 1, HALF + n] = 1.0
    return matrices, by_row, by_lane, np.stack([order.T, order]).astype(ml_dtypes.bfloat16)


def lanes(rows):
    return lax.broadcasted_iota(jnp.int32, (rows, HALF), 1)


def rows_of(first, rows):
    return first + lax.broadcasted_iota(jnp.int32, (rows, HALF), 0)


def swap(x):
    return pltpu.roll(x, HALO, 1)


def split(x):
    high = x.astype(BF16)
    return high, (x - high.astype(F32)).astype(BF16)


def mul(ar, ai, br, bi):
    return ar * br - ai * bi, ar * bi + ai * br


def mul_conj(ar, ai, br, bi):
    return ar * br + ai * bi, ar * bi - ai * br


def dot(a, b):
    return jnp.dot(a, b, preferred_element_type=F32)


def pack_left(re0, im0):
    low = lanes(re0.shape[0]) < HALO
    return jnp.where(low, re0, swap(im0))


def pack_right(re1, im1):
    low = lanes(re1.shape[0]) < HALO
    return jnp.where(low, swap(im1), re1)


def pack_kernel(core_ref, object_ref, top, bottom, out_first, out_last, out_top, out_bottom, in_rows):
    core = core_ref[0]
    for s in range(4):
        for c in range(2):
            top[c, s] = object_ref[c, s, :HALO, :]
            bottom[c, s] = object_ref[c, s, W - HALO :, :]
        for r in range(0, W, 64):
            re, im = object_ref[0, s, r : r + 64, :], object_ref[1, s, r : r + 64, :]
            left = pack_left(re[:, :HALF], im[:, :HALF])
            right = pack_right(re[:, HALF:], im[:, HALF:])
            packed = jnp.where(core == 1, right, left)
            in_rows[s, r : r + 64, :] = jnp.where(core == 1, left, right)
            if s < PARTED:
                out_first[s, r : r + 64, :] = packed
            else:
                out_last[s - PARTED, r : r + 64, :] = packed
            if r == 0:
                out_top[s] = packed
            if r == W - HALO:
                out_bottom[s] = packed


def relay_kernel(core_ref, below_ref, above_ref, last_ref, first_ref, corner_below, corner_above, measured, inward, last):
    core = core_ref[0]
    last[...] = last_ref[...]
    for s in range(4):
        for at, ref in ((0, below_ref), (HALO, above_ref)):
            re, im = ref[0, s], ref[1, s]
            left = pack_left(re[:, :HALF], im[:, :HALF])
            right = pack_right(re[:, HALF:], im[:, HALF:])
            inward[s, at : at + HALO, :] = jnp.where(core == 1, left, right)


def prepare(pos_ref, probe_ref, propagator_ref, intensity_ref, order_ref, wave_ref, phase_ref, measured_ref):
    for k in range(2):
        a = lax.rem(pos_ref[k, 0] + (W - HALO), W)
        b = lax.rem(pos_ref[k, 1] + (W - HALO), W)
        for c in range(2):
            wave_ref[0, k, c] = pltpu.roll(pltpu.roll(probe_ref[c], a, 0), b, 1)

    def ordered(x):
        for left in (True, False):
            total = None
            for _ in range(3):
                part = x.astype(BF16)
                x = x - part.astype(F32)
                term = dot(order_ref[0], part) if left else dot(part, order_ref[1])
                total = term if total is None else total + term
            x = total
        return x

    angle = ordered(propagator_ref[...])
    phase_ref[0] = jnp.cos(angle)
    phase_ref[1] = jnp.sin(angle)
    for k in range(2):
        measured_ref[k] = ordered(intensity_ref[k])


STEP = 32


class Transform:
    def __init__(self, tables, scratch):
        self.matrices, self.by_row, self.by_lane = tables
        self.xr_h, self.xr_l, self.xl_h, self.xl_l, self.wr, self.wl = scratch

    def put_rows(self, k, e, r, re, im):
        cols = slice(e * W, (e + 1) * W)
        n = re.shape[0]
        for base, x in ((0, re), (HALF, im)):
            high, low = split(x)
            self.xr_h[k, base + r : base + r + n, cols] = high
            self.xr_l[k, base + r : base + r + n, cols] = low

    def put_lanes(self, k, e, r, re, im):
        n = re.shape[0]
        for base, x in ((0, re), (HALF, im)):
            high, low = split(x)
            self.xl_h[k, e * W + r : e * W + r + n, base : base + HALF] = high
            self.xl_l[k, e * W + r : e * W + r + n, base : base + HALF] = low

    def enter(self, k, r, n, first, second):
        c = jnp.concatenate([self.by_row[0, r : r + n, :]] * 2, axis=1)
        s = jnp.concatenate([self.by_row[1, r : r + n, :]] * 2, axis=1)
        self.put_rows(k, 0, r, first[0] + second[0], first[1] + second[1])
        dr, di = first[0] - second[0], first[1] - second[1]
        self.put_rows(k, 1, r, dr * c + di * s, di * c - dr * s)

    def dot_rows(self, k, inverse):
        high, low = self.matrices[2 * inverse], self.matrices[2 * inverse + 1]
        for cols in (slice(0, W), slice(W, 2 * W)):
            xh, xl = self.xr_h[k, :, cols], self.xr_l[k, :, cols]
            self.wr[k, :, cols] = dot(high, xh) + dot(high, xl) + dot(low, xh)

    def dot_lanes(self, k, inverse):
        high, low = self.matrices[2 - 2 * inverse], self.matrices[3 - 2 * inverse]
        for rows in (slice(0, W), slice(W, 2 * W)):
            xh, xl = self.xl_h[k, rows], self.xl_l[k, rows]
            self.wl[k, rows] = dot(xh, high) + dot(xl, high) + dot(xh, low)

    def along_lanes(self, k):
        for e in range(2):
            cols = slice(e * W, (e + 1) * W)
            for r in range(0, HALF, STEP):
                n = STEP
                re = self.wr[k, r : r + n, cols]
                im = self.wr[k, HALF + r : HALF + r + n, cols]
                row = e * HALF + r
                c = jnp.concatenate([self.by_lane[0]] * (n // 8), axis=0)
                s = jnp.concatenate([self.by_lane[1]] * (n // 8), axis=0)
                re0, re1, im0, im1 = re[:, :HALF], re[:, HALF:], im[:, :HALF], im[:, HALF:]
                self.put_lanes(k, 0, row, re0 + re1, im0 + im1)
                dr, di = re0 - re1, im0 - im1
                self.put_lanes(k, 1, row, dr * c + di * s, di * c - dr * s)

    def modify(self, k, change):
        for e in range(2):
            for r in range(0, W, STEP):
                n = STEP
                rows = slice(e * W + r, e * W + r + n)
                re, im = change(e, slice(r, r + n), self.wl[k, rows, :HALF], self.wl[k, rows, HALF:])
                self.put_lanes(k, e, r, re, im)

    def back_along_lanes(self, k):
        for e in range(2):
            for r in range(0, HALF, STEP):
                n = STEP
                row = e * HALF + r
                c = jnp.concatenate([self.by_lane[0]] * (n // 8), axis=0)
                s = jnp.concatenate([self.by_lane[1]] * (n // 8), axis=0)
                er, ei = self.wl[k, row : row + n, :HALF], self.wl[k, row : row + n, HALF:]
                tr, ti = self.wl[k, W + row : W + row + n, :HALF], self.wl[k, W + row : W + row + n, HALF:]
                tr, ti = tr * c - ti * s, ti * c + tr * s
                re = jnp.concatenate([er + tr, er - tr], axis=1)
                im = jnp.concatenate([ei + ti, ei - ti], axis=1)
                self.put_rows(k, e, r, re, im)

    def around(self, entering, changes):
        for k in range(2):
            entering(k)
            self.dot_rows(k, 0)
        for k in range(2):
            self.along_lanes(k)
            self.dot_lanes(k, 0)
        for k in range(2):
            self.modify(k, changes[k])
            self.dot_lanes(k, 1)
        for k in range(2):
            self.back_along_lanes(k)
            self.dot_rows(k, 1)

    def leave(self, k, r, n):
        c = jnp.concatenate([self.by_row[0, r : r + n, :]] * 2, axis=1)
        s = jnp.concatenate([self.by_row[1, r : r + n, :]] * 2, axis=1)
        er, ei = self.wr[k, r : r + n, :W], self.wr[k, HALF + r : HALF + r + n, :W]
        tr, ti = self.wr[k, r : r + n, W:], self.wr[k, HALF + r : HALF + r + n, W:]
        tr, ti = tr * c - ti * s, ti * c + tr * s
        return (er + tr, ei + ti), (er - tr, ei - ti)


def phase_of(phase_ref, sign):
    def change(e, rows, re, im):
        cols = slice(e * HALF, (e + 1) * HALF)
        pr, pi = phase_ref[0, rows, cols], phase_ref[1, rows, cols]
        return mul(re, im, pr, pi) if sign > 0 else mul_conj(pr, pi, re, im)

    return change


def misfit_of(measured_ref, k):
    def change(e, rows, re, im):
        cols = slice(e * HALF, (e + 1) * HALF)
        misfit = re * re + im * im - measured_ref[k, rows, cols]
        return misfit * re, misfit * im

    return change


class Windows:
    def __init__(self, pos_ref, core_ref, refs, side, at):
        self.at = at
        self.core = core_ref[0]
        self.object, self.below, self.above, self.out, self.out_below, self.out_above, self.inner, self.in_rows = refs
        self.side = side
        self.shift = [(pos_ref[k, 0] - HALO, pos_ref[k, 1] - HALO) for k in range(2)]

    def gather_sides(self, s):
        for r in range(0, 384, 64):
            if r < W:
                outer = self.out[s - self.at, r : r + 64]
            else:
                outer = (self.out_below if r == W else self.out_above)[s]
            inner = self.in_rows[s, r : r + 64] if r < W else self.inner[s, r - W : r - W + 64]
            right = jnp.where(self.core == 1, outer, inner)
            left = jnp.where(self.core == 1, inner, outer)
            low = lanes(64) < HALO
            self.side[0, r : r + 64] = jnp.where(low, right, left)
            self.side[1, r : r + 64] = swap(jnp.where(low, left, right))

    def with_sides(self, k, own, side):
        b = self.shift[k][1]
        lane = lanes(own.shape[0])
        return (
            jnp.where(lane < b, side, own[:, :HALF]),
            jnp.where(lane >= HALF + b, side, own[:, HALF:]),
        )

    def window(self, s, k, c, r, n):
        tiles = self.with_sides(k, self.object[c, s, r : r + n, :], self.side[c, r : r + n])
        a = self.shift[k][0]
        if r < HALO:
            other = self.with_sides(k, self.below[c, s, r : r + n, :], self.side[c, W + r : W + r + n])
            wraps = rows_of(r, n) < a
        elif r >= W - HALO:
            q = r - (W - HALO)
            other = self.with_sides(k, self.above[c, s, q : q + n, :], self.side[c, W + HALO + q : W + HALO + q + n])
            wraps = rows_of(r, n) >= W + a
        else:
            return jnp.concatenate(tiles, axis=1)
        return jnp.concatenate([jnp.where(wraps, o, t) for t, o in zip(tiles, other)], axis=1)


class Folding:
    def __init__(self, pos_ref, core_ref, refs, at):
        self.at = at
        self.core = core_ref[0]
        self.own, self.below, self.above, self.out, self.out_below, self.out_above, self.inner = refs
        self.shift = [(pos_ref[k, 0] - HALO, pos_ref[k, 1] - HALO) for k in range(2)]

    def part(self, terms, keep):
        n = terms[0].shape[0]
        lane = lanes(n)
        tiles, sides = [0.0, 0.0], 0.0
        for k, term in enumerate(terms):
            b = self.shift[k][1]
            zero = jnp.zeros((n, HALF), F32)
            for t, wraps in enumerate((lane < b, lane >= HALF + b)):
                x = term[:, t * HALF : (t + 1) * HALF]
                if keep is not None:
                    x = jnp.where(keep[k], x, zero)
                tiles[t] = tiles[t] + jnp.where(wraps, zero, x)
                sides = sides + jnp.where(wraps, x, zero)
        return jnp.concatenate(tiles, axis=1), sides

    def sides_to(self, j, r, n, re, im, out):
        low = lanes(n) < HALO
        flipped = swap(im)
        right = jnp.where(low, re, flipped)
        left = jnp.where(low, flipped, re)
        ref, i, at = out
        ref[i, at : at + n] = jnp.where(self.core == 1, right, left)
        self.inner[j, r : r + n] = jnp.where(self.core == 1, left, right)

    def put(self, j, r, terms):
        n = terms[0][0].shape[0]
        if HALO <= r < W - HALO:
            parts = [self.part(terms[c], None) for c in range(2)]
        else:
            row = rows_of(r, n)
            if r < HALO:
                wraps = [row < self.shift[k][0] for k in range(2)]
                band, out, at, q = self.below, self.out_below, r, W + r
            else:
                wraps = [row >= W + self.shift[k][0] for k in range(2)]
                at = r - (W - HALO)
                band, out, q = self.above, self.out_above, W + HALO + at
            away = [self.part(terms[c], wraps) for c in range(2)]
            for c in range(2):
                band[c, j, at : at + n, :] = away[c][0]
            self.sides_to(j, q, n, away[0][1], away[1][1], (out, j, at))
            stays = [jnp.logical_not(w) for w in wraps]
            parts = [self.part(terms[c], stays) for c in range(2)]
        for c in range(2):
            self.own[c, j, r : r + n, :] = parts[c][0]
        self.sides_to(j, r, n, parts[0][1], parts[1][1], (self.out, j - self.at, r))


PAIRS = [(r, STEP) for r in range(0, HALF, STEP)]


def forward_slices(t, w, waves, seen, phase, low, high):
    def slice_step(s, carry):
        w.gather_sides(s)

        def entering(k):
            for r, n in PAIRS:
                exits = []
                for q in (r, r + HALF):
                    o = [w.window(s, k, c, q, n) for c in range(2)]
                    for c in range(2):
                        seen[s, k, c, q : q + n, :] = o[c]
                    exits.append(mul(waves[s, k, 0, q : q + n, :], waves[s, k, 1, q : q + n, :], *o))
                t.enter(k, r, n, *exits)

        t.around(entering, [phase_of(phase, 1)] * 2)
        for k in range(2):
            for r, n in PAIRS:
                for q, pair in zip((r, r + HALF), t.leave(k, r, n)):
                    for c in range(2):
                        waves[s + 1, k, c, q : q + n, :] = pair[c]
        return carry

    lax.fori_loop(low, high, slice_step, 0)


def collect(t, f, waves, seen, back, s):
    for r, n in PAIRS:
        pairs = [t.leave(k, r, n) for k in range(2)]
        for half, q in enumerate((r, r + HALF)):
            terms = [[], []]
            for k in range(2):
                g = pairs[k][half]
                wave = waves[s, k, 0, q : q + n, :], waves[s, k, 1, q : q + n, :]
                for c, x in enumerate(mul_conj(*wave, *g)):
                    terms[c].append(x)
                o = seen[s, k, 0, q : q + n, :], seen[s, k, 1, q : q + n, :]
                back[k, 0, q : q + n, :], back[k, 1, q : q + n, :] = mul_conj(*o, *g)
            f.put(s, q, terms)


def backward_slices(t, f, waves, seen, phase, back, high, low):
    def slice_step(i, carry):
        s = high - 1 - i

        def entering(k):
            for r, n in PAIRS:
                t.enter(k, r, n, *[(back[k, 0, q : q + n, :], back[k, 1, q : q + n, :]) for q in (r, r + HALF)])

        t.around(entering, [phase_of(phase, -1)] * 2)
        collect(t, f, waves, seen, back, s)
        return carry

    lax.fori_loop(0, high - low, slice_step, 0)


def forward_kernel(pos, core, waves_in, phase, obj, below, above, out, out_below, out_above, inner, in_rows,
                   mats, by_row, by_lane, waves, seen, xr_h, xr_l, xl_h, xl_l, wr, wl, side):
    t = Transform((mats, by_row, by_lane), (xr_h, xr_l, xl_h, xl_l, wr, wl))
    w = Windows(pos, core, (obj, below, above, out, out_below, out_above, inner, in_rows), side, 0)
    forward_slices(t, w, waves, seen, phase, 0, PARTED)


def turn_kernel(pos, core, waves_in, seen_in, phase, measured, obj, below, above, out, out_below, out_above, inner,
                in_rows, mats, by_row, by_lane,
                waves, seen, back, own, g_below, g_above, g_out_below, g_out_above, g_inner, g_out,
                xr_h, xr_l, xl_h, xl_l, wr, wl, side):
    t = Transform((mats, by_row, by_lane), (xr_h, xr_l, xl_h, xl_l, wr, wl))
    w = Windows(pos, core, (obj, below, above, out, out_below, out_above, inner, in_rows), side, PARTED)
    f = Folding(pos, core, (own, g_below, g_above, g_out, g_out_below, g_out_above, g_inner), PARTED)
    forward_slices(t, w, waves, seen, phase, PARTED, 3)
    w.gather_sides(3)

    def entering(k):
        for r, n in PAIRS:
            exits = []
            for q in (r, r + HALF):
                o = [w.window(3, k, c, q, n) for c in range(2)]
                for c in range(2):
                    seen[3, k, c, q : q + n, :] = o[c]
                exits.append(mul(waves[3, k, 0, q : q + n, :], waves[3, k, 1, q : q + n, :], *o))
            t.enter(k, r, n, *exits)

    t.around(entering, [misfit_of(measured, k) for k in range(2)])
    collect(t, f, waves, seen, back, 3)
    backward_slices(t, f, waves, seen, phase, back, 3, PARTED)


def backward_kernel(pos, core, back_in, waves, seen, phase, own_in, g_below_in, g_above_in, g_out_below_in, g_out_above_in,
                    g_inner_in, mats, by_row, by_lane,
                    back, own, g_below, g_above, g_out_below, g_out_above, g_inner, g_out,
                    xr_h, xr_l, xl_h, xl_l, wr, wl):
    t = Transform((mats, by_row, by_lane), (xr_h, xr_l, xl_h, xl_l, wr, wl))
    f = Folding(pos, core, (own, g_below, g_above, g_out, g_out_below, g_out_above, g_inner), 0)
    backward_slices(t, f, waves, seen, phase, back, PARTED, 0)


def spread(core, outer, inner):
    low = lanes(outer.shape[0]) < HALO
    zero = jnp.zeros(outer.shape, F32)
    left = jnp.where(core == 1, inner, outer)
    right = jnp.where(core == 1, outer, inner)
    left_im, right_im = swap(left), swap(right)
    re = jnp.concatenate([jnp.where(low, left, zero), jnp.where(low, zero, right)], axis=1)
    im = jnp.concatenate([jnp.where(low, left_im, zero), jnp.where(low, zero, right_im)], axis=1)
    return re, im


def bands_kernel(core_ref, g_below, g_above, inner, out_last, to_below, to_above):
    core = core_ref[0]
    for s in range(4):
        for at, source, target in ((W, g_below, to_below), (W + HALO, g_above, to_above)):
            part = inner[s, at : at + HALO]
            more = spread(core, jnp.zeros_like(part), part)
            for c in range(2):
                target[c, s] = source[c, s] + more[c]


def final_kernel(core_ref, obj, own, from_above, from_below, out_first, out_last, out_above, out_below, inner,
                 gradient_out, updated_out, gradient, updated, sent):
    core = core_ref[0]
    copies = []
    for s in range(4):
        out, j = (out_first, s) if s < PARTED else (out_last, s - PARTED)
        for r in range(0, W, 64):
            side = out[j, r : r + 64]
            if r == 0:
                side = side + out_above[s]
            if r == W - HALO:
                side = side + out_below[s]
            more = spread(core, side, inner[s, r : r + 64])
            for c in range(2):
                total = own[c, s, r : r + 64, :] + more[c]
                if r == 0:
                    total = total + from_above[c, s]
                if r == W - HALO:
                    total = total + from_below[c, s]
                gradient[s, c, r : r + 64, :] = total
                updated[s, c, r : r + 64, :] = obj[c, s, r : r + 64, :] - RATE * total
        for i, (held, target) in enumerate(((gradient, gradient_out), (updated, updated_out))):
            copies.append(pltpu.make_async_copy(held.at[s], target.at[:, s], sent.at[2 * s + i]))
            copies[-1].start()
    for copy in copies:
        copy.wait()


SMEM = pl.BlockSpec(memory_space=pltpu.SMEM)
VMEM = pl.BlockSpec(memory_space=pltpu.VMEM)
ANYWHERE = pl.BlockSpec(memory_space=pl.ANY)
HBM = pl.BlockSpec(memory_space=pltpu.HBM)


def call(kernel, outs, args, scalars, scratch=(), flops=0, moved=2**20, limit=24, aliases=None, places=None, targets=None):
    shapes = [jax.ShapeDtypeStruct(shape, F32) for shape in outs]
    return pl.pallas_call(
        kernel,
        out_shape=shapes,
        in_specs=[SMEM] * scalars + (places or [VMEM] * (len(args) - scalars)),
        out_specs=targets or [VMEM] * len(shapes),
        scratch_shapes=list(scratch),
        input_output_aliases=aliases or {},
        compiler_params=pltpu.CompilerParams(vmem_limit_bytes=limit * 1024 * 1024),
        cost_estimate=pl.CostEstimate(flops=flops, bytes_accessed=moved, transcendentals=0),
    )(*args)


TRANSFORM_SCRATCH = [
    pltpu.VMEM((2, W, 2 * W), BF16),
    pltpu.VMEM((2, W, 2 * W), BF16),
    pltpu.VMEM((2, 2 * W, W), BF16),
    pltpu.VMEM((2, 2 * W, W), BF16),
    pltpu.VMEM((2, W, 2 * W), F32),
    pltpu.VMEM((2, 2 * W, W), F32),
]
SIDE_SCRATCH = pltpu.VMEM((2, 384, HALF), F32)
STACK = (4, 2, 2, W, W)


def routes(rows, cols):
    def out(c):
        return c + 1 if c % 2 else c - 1

    def build(step, col):
        return [
            (r * cols + c, (r + step) % rows * cols + col(c) % cols) for r in range(rows) for c in range(cols)
        ]

    return {
        "up": build(-1, lambda c: c),
        "down": build(1, lambda c: c),
        "out": build(0, out),
        "out_up": build(-1, out),
        "out_down": build(1, out),
        "in": build(0, lambda c: c - 1 if c % 2 else c + 1),
    }


def on_device(obj, positions, intensities, probe, propagator, *, route):
    matrices, by_row, by_lane, order = (jnp.asarray(x) for x in fourier_tables())
    tables = (matrices, by_row, by_lane)
    core = (lax.axis_index("col") % 2).astype(jnp.int32).reshape(1)
    pos = positions[0, 0]
    flops = 2 * 2 * 8 * 3 * 2 * W**3 // 2
    bands, corners, columns, both = (2, 4, HALO, W), (4, HALO, HALF), (4, W, HALF), (4, 2 * HALO, HALF)
    first, last = (PARTED, W, HALF), (4 - PARTED, W, HALF)

    def send(x, way):
        return lax.ppermute(x, AXES, route[way])

    top, bottom, out_first, out_last, out_top, out_bottom, in_rows = call(
        pack_kernel, [bands, bands, first, last, corners, corners, columns], (core, obj), 1
    )
    waves, phase, measured = call(
        prepare,
        [STACK, (2, W, W), (2, W, W)],
        (pos, probe, propagator, intensities[0, 0], order),
        1,
    )
    in_rows, out_bottom = lax.optimization_barrier((send(in_rows, "in"), out_bottom))
    below, above = send(top, "up"), send(bottom, "down")
    out_first = send(out_first, "out")
    corner_below, corner_above = send(out_top, "out_up"), send(out_bottom, "out_down")
    inward, out_last = call(
        relay_kernel,
        [both, last],
        (core, below, above, out_last, out_first, corner_below, corner_above, measured),
        1,
        places=[VMEM] * 3 + [ANYWHERE] * 4,
    )
    out_last = send(out_last, "out")
    inner = send(inward, "in")

    waves, seen = call(
        forward_kernel,
        [STACK, STACK],
        (pos, core, waves, phase, obj, below, above, out_first, corner_below, corner_above, inner, in_rows, *tables),
        2,
        TRANSFORM_SCRATCH + [SIDE_SCRATCH],
        flops=PARTED * flops,
        aliases={2: 0},
    )
    sums = [(2, 4, W, W), bands, bands, corners, corners, (4, 384, HALF)]
    waves, seen, back, *terms, out_last = call(
        turn_kernel,
        [STACK, STACK, (2, 2, W, W), *sums, last],
        (pos, core, waves, seen, phase, measured, obj, below, above, out_last, corner_below, corner_above, inner, in_rows, *tables),
        2,
        TRANSFORM_SCRATCH + [SIDE_SCRATCH],
        flops=(7 - 2 * PARTED) * flops,
        aliases={2: 0, 3: 1},
    )
    out_last = send(out_last, "out")
    _, own, g_below, g_above, g_out_below, g_out_above, g_inner, out_first = call(
        backward_kernel,
        [(2, 2, W, W), *sums, first],
        (pos, core, back, waves, seen, phase, *terms, *tables),
        2,
        TRANSFORM_SCRATCH,
        flops=PARTED * flops,
        aliases={2: 0, **{6 + i: 1 + i for i in range(6)}},
    )

    g_inner, out_last = lax.optimization_barrier((g_inner, out_last))
    inner = send(g_inner, "in")
    out_first = send(out_first, "out")
    out_above = send(g_out_below, "out_down")
    out_below = send(g_out_above, "out_up")
    to_below, to_above = call(
        bands_kernel, [bands, bands], (core, g_below, g_above, inner, out_last), 1, places=[VMEM] * 3 + [ANYWHERE]
    )
    from_above = send(to_below, "down")
    from_below = send(to_above, "up")
    return tuple(
        call(
            final_kernel,
            [(2, 4, W, W)] * 2,
            (core, obj, own, from_above, from_below, out_first, out_last, out_above, out_below, inner),
            1,
            [pltpu.VMEM((4, 2, W, W), F32), pltpu.VMEM((4, 2, W, W), F32), pltpu.SemaphoreType.DMA((8,))],
            targets=[HBM] * 2,
        )
    )


def solution(mesh):
    route = routes(mesh.shape["row"], mesh.shape["col"])
    return jax.shard_map(
        functools.partial(on_device, route=route),
        mesh=mesh,
        in_specs=(
            P(None, None, "row", "col"),
            P("row", "col", None, None),
            P("row", "col", None, None, None),
            P(),
            P(),
        ),
        out_specs=(P(None, None, "row", "col"), P(None, None, "row", "col")),
        check_vma=False,
    )
```

```python
import functools

import jax
import jax.numpy as jnp
import ml_dtypes
import numpy as np
from jax import lax
from jax.experimental import pallas as pl
from jax.experimental.pallas import tpu as pltpu
from jax.sharding import PartitionSpec as P

HALO = 64
W = 256
HALF = 128
F32 = jnp.float32
BF16 = jnp.bfloat16
AXES = ("row", "col")
RATE = 0.5
PARTED = 2


def fourier_tables():
    n = np.arange(HALF)
    angle = 2.0 * np.pi * (np.outer(n, n) % HALF) / HALF
    cos, sin = np.cos(angle) / 16.0, np.sin(angle) / 16.0
    forward = np.block([[cos, sin], [-sin, cos]]).astype(np.float32)
    both = []
    for matrix in (forward, forward.T):
        high = matrix.astype(ml_dtypes.bfloat16)
        low = (matrix - high.astype(np.float32)).astype(ml_dtypes.bfloat16)
        both += [high, low]
    matrices = np.stack(both)
    turn = 2.0 * np.pi * n / W
    twiddle = np.stack([np.cos(turn), np.sin(turn)]).astype(np.float32)
    by_row = np.broadcast_to(twiddle[:, :, None], (2, HALF, HALF)).copy()
    by_lane = np.broadcast_to(twiddle[:, None, :], (2, 8, HALF)).copy()
    order = np.zeros((W, W), np.float32)
    order[2 * n, n] = 1.0
    order[2 * n + 1, HALF + n] = 1.0
    return matrices, by_row, by_lane, np.stack([order.T, order]).astype(ml_dtypes.bfloat16)


def lanes(rows):
    return lax.broadcasted_iota(jnp.int32, (rows, HALF), 1)


def rows_of(first, rows):
    return first + lax.broadcasted_iota(jnp.int32, (rows, HALF), 0)


def swap(x):
    return pltpu.roll(x, HALO, 1)


def split(x):
    high = x.astype(BF16)
    return high, (x - high.astype(F32)).astype(BF16)


def mul(ar, ai, br, bi):
    return ar * br - ai * bi, ar * bi + ai * br


def mul_conj(ar, ai, br, bi):
    return ar * br + ai * bi, ar * bi - ai * br


def dot(a, b):
    return jnp.dot(a, b, preferred_element_type=F32)


def pack_left(re0, im0):
    low = lanes(re0.shape[0]) < HALO
    return jnp.where(low, re0, swap(im0))


def pack_right(re1, im1):
    low = lanes(re1.shape[0]) < HALO
    return jnp.where(low, swap(im1), re1)


def pack_kernel(core_ref, object_ref, top, bottom, out_first, out_last, out_top, out_bottom, band, arrived):
    core = core_ref[0]
    lane = pl.multiple_of(core * HALF, HALF)
    rows = [
        pltpu.make_async_copy(object_ref.at[:, :, :HALO], top, arrived.at[0]),
        pltpu.make_async_copy(object_ref.at[:, :, W - HALO :], bottom, arrived.at[1]),
    ]
    columns = pltpu.make_async_copy(object_ref.at[:, :, :, pl.ds(lane, HALF)], band, arrived.at[2])
    columns.start()
    for copy in rows:
        copy.start()
    columns.wait()
    for s in range(4):
        for r in range(0, W, 64):
            re, im = band[0, s, r : r + 64], band[1, s, r : r + 64]
            packed = jnp.where(core == 1, pack_right(re, im), pack_left(re, im))
            if s < PARTED:
                out_first[s, r : r + 64, :] = packed
            else:
                out_last[s - PARTED, r : r + 64, :] = packed
            if r == 0:
                out_top[s] = packed
            if r == W - HALO:
                out_bottom[s] = packed
    for copy in rows:
        copy.wait()


def relay_kernel(core_ref, object_ref, below_ref, above_ref, last_ref, first_ref, corner_below, corner_above, measured,
                 inward, last):
    core = core_ref[0]
    last[...] = last_ref[...]
    for s in range(4):
        for r in range(0, 384, 64):
            if r < W:
                re, im = object_ref[0, s, r : r + 64], object_ref[1, s, r : r + 64]
            else:
                ref = below_ref if r == W else above_ref
                re, im = ref[0, s], ref[1, s]
            left = pack_left(re[:, :HALF], im[:, :HALF])
            right = pack_right(re[:, HALF:], im[:, HALF:])
            inward[s, r : r + 64, :] = jnp.where(core == 1, left, right)


def prepare(pos_ref, probe_ref, propagator_ref, intensity_ref, order_ref, wave_ref, phase_ref, measured_ref):
    for k in range(2):
        a = lax.rem(pos_ref[k, 0] + (W - HALO), W)
        b = lax.rem(pos_ref[k, 1] + (W - HALO), W)
        for c in range(2):
            wave_ref[0, k, c] = pltpu.roll(pltpu.roll(probe_ref[c], a, 0), b, 1)

    def ordered(x):
        for left in (True, False):
            total = None
            for _ in range(3):
                part = x.astype(BF16)
                x = x - part.astype(F32)
                term = dot(order_ref[0], part) if left else dot(part, order_ref[1])
                total = term if total is None else total + term
            x = total
        return x

    angle = ordered(propagator_ref[...])
    phase_ref[0] = jnp.cos(angle)
    phase_ref[1] = jnp.sin(angle)
    for k in range(2):
        measured_ref[k] = ordered(intensity_ref[k])


STEP = 32


class Transform:
    def __init__(self, tables, scratch):
        self.matrices, self.by_row, self.by_lane = tables
        self.xr_h, self.xr_l, self.xl_h, self.xl_l, self.wr, self.wl = scratch

    def put_rows(self, k, e, r, re, im):
        cols = slice(e * W, (e + 1) * W)
        n = re.shape[0]
        for base, x in ((0, re), (HALF, im)):
            high, low = split(x)
            self.xr_h[k, base + r : base + r + n, cols] = high
            self.xr_l[k, base + r : base + r + n, cols] = low

    def put_lanes(self, k, e, r, re, im):
        n = re.shape[0]
        for base, x in ((0, re), (HALF, im)):
            high, low = split(x)
            self.xl_h[k, e * W + r : e * W + r + n, base : base + HALF] = high
            self.xl_l[k, e * W + r : e * W + r + n, base : base + HALF] = low

    def enter(self, k, r, n, first, second):
        c = jnp.concatenate([self.by_row[0, r : r + n, :]] * 2, axis=1)
        s = jnp.concatenate([self.by_row[1, r : r + n, :]] * 2, axis=1)
        self.put_rows(k, 0, r, first[0] + second[0], first[1] + second[1])
        dr, di = first[0] - second[0], first[1] - second[1]
        self.put_rows(k, 1, r, dr * c + di * s, di * c - dr * s)

    def dot_rows(self, k, inverse):
        high, low = self.matrices[2 * inverse], self.matrices[2 * inverse + 1]
        for cols in (slice(0, W), slice(W, 2 * W)):
            xh, xl = self.xr_h[k, :, cols], self.xr_l[k, :, cols]
            self.wr[k, :, cols] = dot(high, xh) + dot(high, xl) + dot(low, xh)

    def dot_lanes(self, k, inverse):
        high, low = self.matrices[2 - 2 * inverse], self.matrices[3 - 2 * inverse]
        for rows in (slice(0, W), slice(W, 2 * W)):
            xh, xl = self.xl_h[k, rows], self.xl_l[k, rows]
            self.wl[k, rows] = dot(xh, high) + dot(xl, high) + dot(xh, low)

    def along_lanes(self, k):
        for e in range(2):
            cols = slice(e * W, (e + 1) * W)
            for r in range(0, HALF, STEP):
                n = STEP
                re = self.wr[k, r : r + n, cols]
                im = self.wr[k, HALF + r : HALF + r + n, cols]
                row = e * HALF + r
                c = jnp.concatenate([self.by_lane[0]] * (n // 8), axis=0)
                s = jnp.concatenate([self.by_lane[1]] * (n // 8), axis=0)
                re0, re1, im0, im1 = re[:, :HALF], re[:, HALF:], im[:, :HALF], im[:, HALF:]
                self.put_lanes(k, 0, row, re0 + re1, im0 + im1)
                dr, di = re0 - re1, im0 - im1
                self.put_lanes(k, 1, row, dr * c + di * s, di * c - dr * s)

    def modify(self, k, change):
        for e in range(2):
            for r in range(0, W, STEP):
                n = STEP
                rows = slice(e * W + r, e * W + r + n)
                re, im = change(e, slice(r, r + n), self.wl[k, rows, :HALF], self.wl[k, rows, HALF:])
                self.put_lanes(k, e, r, re, im)

    def back_along_lanes(self, k):
        for e in range(2):
            for r in range(0, HALF, STEP):
                n = STEP
                row = e * HALF + r
                c = jnp.concatenate([self.by_lane[0]] * (n // 8), axis=0)
                s = jnp.concatenate([self.by_lane[1]] * (n // 8), axis=0)
                er, ei = self.wl[k, row : row + n, :HALF], self.wl[k, row : row + n, HALF:]
                tr, ti = self.wl[k, W + row : W + row + n, :HALF], self.wl[k, W + row : W + row + n, HALF:]
                tr, ti = tr * c - ti * s, ti * c + tr * s
                re = jnp.concatenate([er + tr, er - tr], axis=1)
                im = jnp.concatenate([ei + ti, ei - ti], axis=1)
                self.put_rows(k, e, r, re, im)

    def around(self, entering, changes):
        for k in range(2):
            entering(k)
            self.dot_rows(k, 0)
        for k in range(2):
            self.along_lanes(k)
            self.dot_lanes(k, 0)
        for k in range(2):
            self.modify(k, changes[k])
            self.dot_lanes(k, 1)
        for k in range(2):
            self.back_along_lanes(k)
            self.dot_rows(k, 1)

    def leave(self, k, r, n):
        c = jnp.concatenate([self.by_row[0, r : r + n, :]] * 2, axis=1)
        s = jnp.concatenate([self.by_row[1, r : r + n, :]] * 2, axis=1)
        er, ei = self.wr[k, r : r + n, :W], self.wr[k, HALF + r : HALF + r + n, :W]
        tr, ti = self.wr[k, r : r + n, W:], self.wr[k, HALF + r : HALF + r + n, W:]
        tr, ti = tr * c - ti * s, ti * c + tr * s
        return (er + tr, ei + ti), (er - tr, ei - ti)


def phase_of(phase_ref, sign):
    def change(e, rows, re, im):
        cols = slice(e * HALF, (e + 1) * HALF)
        pr, pi = phase_ref[0, rows, cols], phase_ref[1, rows, cols]
        return mul(re, im, pr, pi) if sign > 0 else mul_conj(pr, pi, re, im)

    return change


def misfit_of(measured_ref, k):
    def change(e, rows, re, im):
        cols = slice(e * HALF, (e + 1) * HALF)
        misfit = re * re + im * im - measured_ref[k, rows, cols]
        return misfit * re, misfit * im

    return change


class Windows:
    def __init__(self, pos_ref, core_ref, refs, side, at):
        self.at = at
        self.core = core_ref[0]
        self.object, self.below, self.above, self.out, self.out_below, self.out_above, self.inner = refs
        self.side = side
        self.shift = [(pos_ref[k, 0] - HALO, pos_ref[k, 1] - HALO) for k in range(2)]

    def gather_sides(self, s):
        for r in range(0, 384, 64):
            if r < W:
                outer = self.out[s - self.at, r : r + 64]
            else:
                outer = (self.out_below if r == W else self.out_above)[s]
            inner = self.inner[s, r : r + 64]
            right = jnp.where(self.core == 1, outer, inner)
            left = jnp.where(self.core == 1, inner, outer)
            low = lanes(64) < HALO
            self.side[0, r : r + 64] = jnp.where(low, right, left)
            self.side[1, r : r + 64] = swap(jnp.where(low, left, right))

    def with_sides(self, k, own, side):
        b = self.shift[k][1]
        lane = lanes(own.shape[0])
        return (
            jnp.where(lane < b, side, own[:, :HALF]),
            jnp.where(lane >= HALF + b, side, own[:, HALF:]),
        )

    def window(self, s, k, c, r, n):
        tiles = self.with_sides(k, self.object[c, s, r : r + n, :], self.side[c, r : r + n])
        a = self.shift[k][0]
        if r < HALO:
            other = self.with_sides(k, self.below[c, s, r : r + n, :], self.side[c, W + r : W + r + n])
            wraps = rows_of(r, n) < a
        elif r >= W - HALO:
            q = r - (W - HALO)
            other = self.with_sides(k, self.above[c, s, q : q + n, :], self.side[c, W + HALO + q : W + HALO + q + n])
            wraps = rows_of(r, n) >= W + a
        else:
            return jnp.concatenate(tiles, axis=1)
        return jnp.concatenate([jnp.where(wraps, o, t) for t, o in zip(tiles, other)], axis=1)


class Folding:
    def __init__(self, pos_ref, core_ref, refs, at):
        self.at = at
        self.core = core_ref[0]
        self.own, self.below, self.above, self.out, self.out_below, self.out_above, self.inner = refs
        self.shift = [(pos_ref[k, 0] - HALO, pos_ref[k, 1] - HALO) for k in range(2)]

    def part(self, terms, keep):
        n = terms[0].shape[0]
        lane = lanes(n)
        tiles, sides = [0.0, 0.0], 0.0
        for k, term in enumerate(terms):
            b = self.shift[k][1]
            zero = jnp.zeros((n, HALF), F32)
            for t, wraps in enumerate((lane < b, lane >= HALF + b)):
                x = term[:, t * HALF : (t + 1) * HALF]
                if keep is not None:
                    x = jnp.where(keep[k], x, zero)
                tiles[t] = tiles[t] + jnp.where(wraps, zero, x)
                sides = sides + jnp.where(wraps, x, zero)
        return jnp.concatenate(tiles, axis=1), sides

    def sides_to(self, j, r, n, re, im, out):
        low = lanes(n) < HALO
        flipped = swap(im)
        right = jnp.where(low, re, flipped)
        left = jnp.where(low, flipped, re)
        ref, i, at = out
        ref[i, at : at + n] = jnp.where(self.core == 1, right, left)
        self.inner[j, r : r + n] = jnp.where(self.core == 1, left, right)

    def put(self, j, r, terms):
        n = terms[0][0].shape[0]
        if HALO <= r < W - HALO:
            parts = [self.part(terms[c], None) for c in range(2)]
        else:
            row = rows_of(r, n)
            if r < HALO:
                wraps = [row < self.shift[k][0] for k in range(2)]
                band, out, at, q = self.below, self.out_below, r, W + r
            else:
                wraps = [row >= W + self.shift[k][0] for k in range(2)]
                at = r - (W - HALO)
                band, out, q = self.above, self.out_above, W + HALO + at
            away = [self.part(terms[c], wraps) for c in range(2)]
            for c in range(2):
                band[c, j, at : at + n, :] = away[c][0]
            self.sides_to(j, q, n, away[0][1], away[1][1], (out, j, at))
            stays = [jnp.logical_not(w) for w in wraps]
            parts = [self.part(terms[c], stays) for c in range(2)]
        for c in range(2):
            self.own[c, j, r : r + n, :] = parts[c][0]
        self.sides_to(j, r, n, parts[0][1], parts[1][1], (self.out, j - self.at, r))


PAIRS = [(r, STEP) for r in range(0, HALF, STEP)]


def forward_slices(t, w, waves, seen, phase, low, high):
    def slice_step(s, carry):
        w.gather_sides(s)

        def entering(k):
            for r, n in PAIRS:
                exits = []
                for q in (r, r + HALF):
                    o = [w.window(s, k, c, q, n) for c in range(2)]
                    for c in range(2):
                        seen[s, k, c, q : q + n, :] = o[c]
                    exits.append(mul(waves[s, k, 0, q : q + n, :], waves[s, k, 1, q : q + n, :], *o))
                t.enter(k, r, n, *exits)

        t.around(entering, [phase_of(phase, 1)] * 2)
        for k in range(2):
            for r, n in PAIRS:
                for q, pair in zip((r, r + HALF), t.leave(k, r, n)):
                    for c in range(2):
                        waves[s + 1, k, c, q : q + n, :] = pair[c]
        return carry

    lax.fori_loop(low, high, slice_step, 0)


def collect(t, f, waves, seen, back, s):
    for r, n in PAIRS:
        pairs = [t.leave(k, r, n) for k in range(2)]
        for half, q in enumerate((r, r + HALF)):
            terms = [[], []]
            for k in range(2):
                g = pairs[k][half]
                wave = waves[s, k, 0, q : q + n, :], waves[s, k, 1, q : q + n, :]
                for c, x in enumerate(mul_conj(*wave, *g)):
                    terms[c].append(x)
                o = seen[s, k, 0, q : q + n, :], seen[s, k, 1, q : q + n, :]
                back[k, 0, q : q + n, :], back[k, 1, q : q + n, :] = mul_conj(*o, *g)
            f.put(s, q, terms)


def backward_slices(t, f, waves, seen, phase, back, high, low):
    def slice_step(i, carry):
        s = high - 1 - i

        def entering(k):
            for r, n in PAIRS:
                t.enter(k, r, n, *[(back[k, 0, q : q + n, :], back[k, 1, q : q + n, :]) for q in (r, r + HALF)])

        t.around(entering, [phase_of(phase, -1)] * 2)
        collect(t, f, waves, seen, back, s)
        return carry

    lax.fori_loop(0, high - low, slice_step, 0)


def forward_kernel(pos, core, waves_in, phase, obj, below, above, out, out_below, out_above, inner, mats, by_row, by_lane,
                   waves, seen, xr_h, xr_l, xl_h, xl_l, wr, wl, side):
    t = Transform((mats, by_row, by_lane), (xr_h, xr_l, xl_h, xl_l, wr, wl))
    w = Windows(pos, core, (obj, below, above, out, out_below, out_above, inner), side, 0)
    forward_slices(t, w, waves, seen, phase, 0, PARTED)


def turn_kernel(pos, core, waves_in, seen_in, phase, measured, obj, below, above, out, out_below, out_above, inner,
                mats, by_row, by_lane,
                waves, seen, back, own, g_below, g_above, g_out_below, g_out_above, g_inner, g_out,
                xr_h, xr_l, xl_h, xl_l, wr, wl, side):
    t = Transform((mats, by_row, by_lane), (xr_h, xr_l, xl_h, xl_l, wr, wl))
    w = Windows(pos, core, (obj, below, above, out, out_below, out_above, inner), side, PARTED)
    f = Folding(pos, core, (own, g_below, g_above, g_out, g_out_below, g_out_above, g_inner), PARTED)
    forward_slices(t, w, waves, seen, phase, PARTED, 3)
    w.gather_sides(3)

    def entering(k):
        for r, n in PAIRS:
            exits = []
            for q in (r, r + HALF):
                o = [w.window(3, k, c, q, n) for c in range(2)]
                for c in range(2):
                    seen[3, k, c, q : q + n, :] = o[c]
                exits.append(mul(waves[3, k, 0, q : q + n, :], waves[3, k, 1, q : q + n, :], *o))
            t.enter(k, r, n, *exits)

    t.around(entering, [misfit_of(measured, k) for k in range(2)])
    collect(t, f, waves, seen, back, 3)
    backward_slices(t, f, waves, seen, phase, back, 3, PARTED)


def backward_kernel(pos, core, back_in, waves, seen, phase, own_in, g_below_in, g_above_in, g_out_below_in, g_out_above_in,
                    g_inner_in, mats, by_row, by_lane,
                    back, own, g_below, g_above, g_out_below, g_out_above, g_inner, g_out,
                    xr_h, xr_l, xl_h, xl_l, wr, wl):
    t = Transform((mats, by_row, by_lane), (xr_h, xr_l, xl_h, xl_l, wr, wl))
    f = Folding(pos, core, (own, g_below, g_above, g_out, g_out_below, g_out_above, g_inner), 0)
    backward_slices(t, f, waves, seen, phase, back, PARTED, 0)


def spread(core, outer, inner):
    low = lanes(outer.shape[0]) < HALO
    zero = jnp.zeros(outer.shape, F32)
    left = jnp.where(core == 1, inner, outer)
    right = jnp.where(core == 1, outer, inner)
    left_im, right_im = swap(left), swap(right)
    re = jnp.concatenate([jnp.where(low, left, zero), jnp.where(low, zero, right)], axis=1)
    im = jnp.concatenate([jnp.where(low, left_im, zero), jnp.where(low, zero, right_im)], axis=1)
    return re, im


def bands_kernel(core_ref, g_below, g_above, inner, out_last, to_below, to_above):
    core = core_ref[0]
    for s in range(4):
        for at, source, target in ((W, g_below, to_below), (W + HALO, g_above, to_above)):
            part = inner[s, at : at + HALO]
            more = spread(core, jnp.zeros_like(part), part)
            for c in range(2):
                target[c, s] = source[c, s] + more[c]


def final_kernel(core_ref, obj, own, from_above, from_below, out_first, out_last, out_above, out_below, inner,
                 gradient_out, updated_out, gradient, updated, sent):
    core = core_ref[0]
    copies = []
    for s in range(4):
        out, j = (out_first, s) if s < PARTED else (out_last, s - PARTED)
        for r in range(0, W, 64):
            side = out[j, r : r + 64]
            if r == 0:
                side = side + out_above[s]
            if r == W - HALO:
                side = side + out_below[s]
            more = spread(core, side, inner[s, r : r + 64])
            for c in range(2):
                total = own[c, s, r : r + 64, :] + more[c]
                if r == 0:
                    total = total + from_above[c, s]
                if r == W - HALO:
                    total = total + from_below[c, s]
                gradient[s, c, r : r + 64, :] = total
                updated[s, c, r : r + 64, :] = obj[c, s, r : r + 64, :] - RATE * total
        for i, (held, target) in enumerate(((gradient, gradient_out), (updated, updated_out))):
            copies.append(pltpu.make_async_copy(held.at[s], target.at[:, s], sent.at[2 * s + i]))
            copies[-1].start()
    for copy in copies:
        copy.wait()


SMEM = pl.BlockSpec(memory_space=pltpu.SMEM)
VMEM = pl.BlockSpec(memory_space=pltpu.VMEM)
ANYWHERE = pl.BlockSpec(memory_space=pl.ANY)
HBM = pl.BlockSpec(memory_space=pltpu.HBM)


def call(kernel, outs, args, scalars, scratch=(), flops=0, moved=2**20, limit=24, aliases=None, places=None, targets=None):
    shapes = [jax.ShapeDtypeStruct(shape, F32) for shape in outs]
    return pl.pallas_call(
        kernel,
        out_shape=shapes,
        in_specs=[SMEM] * scalars + (places or [VMEM] * (len(args) - scalars)),
        out_specs=targets or [VMEM] * len(shapes),
        scratch_shapes=list(scratch),
        input_output_aliases=aliases or {},
        compiler_params=pltpu.CompilerParams(vmem_limit_bytes=limit * 1024 * 1024),
        cost_estimate=pl.CostEstimate(flops=flops, bytes_accessed=moved, transcendentals=0),
    )(*args)


TRANSFORM_SCRATCH = [
    pltpu.VMEM((2, W, 2 * W), BF16),
    pltpu.VMEM((2, W, 2 * W), BF16),
    pltpu.VMEM((2, 2 * W, W), BF16),
    pltpu.VMEM((2, 2 * W, W), BF16),
    pltpu.VMEM((2, W, 2 * W), F32),
    pltpu.VMEM((2, 2 * W, W), F32),
]
SIDE_SCRATCH = pltpu.VMEM((2, 384, HALF), F32)
STACK = (4, 2, 2, W, W)


def routes(rows, cols):
    def out(c):
        return c + 1 if c % 2 else c - 1

    def build(step, col):
        return [
            (r * cols + c, (r + step) % rows * cols + col(c) % cols) for r in range(rows) for c in range(cols)
        ]

    return {
        "up": build(-1, lambda c: c),
        "down": build(1, lambda c: c),
        "out": build(0, out),
        "out_up": build(-1, out),
        "out_down": build(1, out),
        "in": build(0, lambda c: c - 1 if c % 2 else c + 1),
    }


def on_device(obj, positions, intensities, probe, propagator, *, route):
    matrices, by_row, by_lane, order = (jnp.asarray(x) for x in fourier_tables())
    tables = (matrices, by_row, by_lane)
    core = (lax.axis_index("col") % 2).astype(jnp.int32).reshape(1)
    pos = positions[0, 0]
    flops = 2 * 2 * 8 * 3 * 2 * W**3 // 2
    bands, corners, columns = (2, 4, HALO, W), (4, HALO, HALF), (4, 384, HALF)
    first, last = (PARTED, W, HALF), (4 - PARTED, W, HALF)

    def send(x, way):
        return lax.ppermute(x, AXES, route[way])

    top, bottom, out_first, out_last, out_top, out_bottom = call(
        pack_kernel,
        [bands, bands, first, last, corners, corners],
        (core, obj),
        1,
        [pltpu.VMEM((2, 4, W, HALF), F32), pltpu.SemaphoreType.DMA((3,))],
        places=[HBM],
    )
    waves, phase, measured = call(
        prepare,
        [STACK, (2, W, W), (2, W, W)],
        (pos, probe, propagator, intensities[0, 0], order),
        1,
    )
    below, above = send(top, "up"), send(bottom, "down")
    out_first = send(out_first, "out")
    corner_below, corner_above = send(out_top, "out_up"), send(out_bottom, "out_down")
    inward, out_last = call(
        relay_kernel,
        [columns, last],
        (core, obj, below, above, out_last, out_first, corner_below, corner_above, measured),
        1,
        places=[VMEM] * 4 + [ANYWHERE] * 4,
    )
    out_last = send(out_last, "out")
    inner = send(inward, "in")

    waves, seen = call(
        forward_kernel,
        [STACK, STACK],
        (pos, core, waves, phase, obj, below, above, out_first, corner_below, corner_above, inner, *tables),
        2,
        TRANSFORM_SCRATCH + [SIDE_SCRATCH],
        flops=PARTED * flops,
        aliases={2: 0},
    )
    sums = [(2, 4, W, W), bands, bands, corners, corners, columns]
    waves, seen, back, *terms, out_last = call(
        turn_kernel,
        [STACK, STACK, (2, 2, W, W), *sums, last],
        (pos, core, waves, seen, phase, measured, obj, below, above, out_last, corner_below, corner_above, inner, *tables),
        2,
        TRANSFORM_SCRATCH + [SIDE_SCRATCH],
        flops=(7 - 2 * PARTED) * flops,
        aliases={2: 0, 3: 1},
    )
    out_last = send(out_last, "out")
    _, own, g_below, g_above, g_out_below, g_out_above, g_inner, out_first = call(
        backward_kernel,
        [(2, 2, W, W), *sums, first],
        (pos, core, back, waves, seen, phase, *terms, *tables),
        2,
        TRANSFORM_SCRATCH,
        flops=PARTED * flops,
        aliases={2: 0, **{6 + i: 1 + i for i in range(6)}},
    )

    g_inner, out_last = lax.optimization_barrier((g_inner, out_last))
    inner = send(g_inner, "in")
    out_first = send(out_first, "out")
    out_above = send(g_out_below, "out_down")
    out_below = send(g_out_above, "out_up")
    to_below, to_above = call(
        bands_kernel, [bands, bands], (core, g_below, g_above, inner, out_last), 1, places=[VMEM] * 3 + [ANYWHERE]
    )
    from_above = send(to_below, "down")
    from_below = send(to_above, "up")
    return tuple(
        call(
            final_kernel,
            [(2, 4, W, W)] * 2,
            (core, obj, own, from_above, from_below, out_first, out_last, out_above, out_below, inner),
            1,
            [pltpu.VMEM((4, 2, W, W), F32), pltpu.VMEM((4, 2, W, W), F32), pltpu.SemaphoreType.DMA((8,))],
            targets=[HBM] * 2,
        )
    )


def solution(mesh):
    route = routes(mesh.shape["row"], mesh.shape["col"])
    return jax.shard_map(
        functools.partial(on_device, route=route),
        mesh=mesh,
        in_specs=(
            P(None, None, "row", "col"),
            P("row", "col", None, None),
            P("row", "col", None, None, None),
            P(),
            P(),
        ),
        out_specs=(P(None, None, "row", "col"), P(None, None, "row", "col")),
        check_vma=False,
    )
```
